32 devices in a mesh: copies: 2 (over y), task: 4 (over z), ops: 4 (over x, core).
Axes of the slice: x: 2, y: 2, z: 4, core: 2. Of those that a mesh axis runs over, the one named last changes fastest.
Arguments:
- psi: bfloat16 [6144, 384], P(('copies', 'task', 'ops')), parts along dimension 0, may hold values from -6 to 6
- left_env: bfloat16 [8, 4, 32, 256, 256], P(('copies', 'ops'), 'task'), parts along dimension 0, may hold values from -0.375 to 0.375
- right_env: bfloat16 [8, 8, 128, 128], P(('copies', 'ops')), parts along dimension 0, may hold values from -0.09375 to 0.09375
- sec_tiles: int32 [8, 4], P('copies'), parts along dimension 0, may hold values from 1 to 2, as said below
- task_sector: int32 [8, 32], P('copies'), parts along dimension 0, may hold values from 0 to 3, as said below
- task_term: int32 [8, 32], P('copies'), parts along dimension 0, may hold values from 0 to 7, as said below
- task_live: int32 [8, 4, 32], P(('copies', 'ops')), parts along dimension 0, may hold values 0 or 1
Outputs:
- sigma: bfloat16 [6144, 384], P(('copies', 'task', 'ops')), parts along dimension 0
The draws below stay inside these ranges and needn't reach their ends.
There are 2 independent parts, one for each index of `copies`. The reference program is written for one: setup_inputs(seed, part) draws one part's arguments, and reference() takes and returns one part's arrays. A program takes and returns all parts, laid end to end along the dimension named above; each array names one. Nothing has to cross between parts.
Inputs may be any that keep to these rules, and one draw needn't show every extreme that they name: `sec_tiles`: each sector owner's 4 sector sizes sum to 6 tiles. `task_sector`: slot k of every task owner holds a task on a sector of sector owner k mod 4; over all task owners and slots, every (sector owner, sector, term) triple with term below 8 appears in exactly one slot. `task_term`: term of each slot, as described for task_sector.
All inputs are finite; a program needn't handle non-finite values. No bound on the sum of `task_live` on one device may be relied on, other than what follows from the above.
Results may differ from the reference program's by a relative error of at most 0.0058.
Values may be sent and summed in bfloat16 or wider, within the bound.
A program may use at most 64 MiB of HBM per device.

```python
import jax
import jax.numpy as jnp
from jax import lax

TILE = 128
SPH = 4
TERMS = 8
MR = 128
NV = 3
HR = 768
SMAX = 256
TPO = 32
N_TASK = 4
N_OPS = 4


def layout(key):
    home_keys = jax.random.split(jax.random.fold_in(key, 11), N_TASK)
    base_tiles = jnp.where(jnp.arange(SPH) < SPH // 2, 2, 1).astype(jnp.int32)
    tile_table = jax.vmap(lambda home_key: jax.random.permutation(home_key, base_tiles))(home_keys)
    ranking = jax.random.permutation(jax.random.fold_in(key, 12), N_TASK).astype(jnp.int32)
    pair_count = TPO // N_TASK
    task_keys = jax.random.split(jax.random.fold_in(key, 13), N_TASK)
    sector_of = (jnp.arange(TPO) // TERMS).astype(jnp.int32)
    term_of = (jnp.arange(TPO) % TERMS).astype(jnp.int32)

    def one_home(task_key, home_tiles):
        jitter = jax.random.permutation(task_key, TPO).astype(jnp.int32)
        scores = (2 - home_tiles[sector_of]) * TPO + jitter
        return jnp.argsort(scores, stable=True).astype(jnp.int32)
    orders = jax.vmap(one_home)(task_keys, tile_table)
    rank_ids = jnp.arange(TPO).astype(jnp.int32)
    owner_at = jnp.broadcast_to(ranking[rank_ids // pair_count][None, :], (N_TASK, TPO))
    slot_at = (rank_ids % pair_count)[None, :] * N_TASK + jnp.arange(N_TASK).astype(jnp.int32)[:, None]
    sector_table = jnp.zeros((N_TASK, TPO), jnp.int32).at[owner_at, slot_at].set(sector_of[orders])
    term_table = jnp.zeros((N_TASK, TPO), jnp.int32).at[owner_at, slot_at].set(term_of[orders])
    return (tile_table, sector_table, term_table)


def draw_sec_tiles(key, part):
    return layout(key)[0]


def draw_task_sector(key, part):
    return layout(key)[1]


def draw_task_term(key, part):
    return layout(key)[2]


def set_ends(drawn, key, low, high):
    index_at = [jax.random.randint(jax.random.fold_in(key, axis), (), 0, length) for axis, length in enumerate(drawn.shape)]
    widest = drawn.shape.index(max(drawn.shape))
    next_to = index_at[:widest] + [(index_at[widest] + 1) % drawn.shape[widest]] + index_at[widest + 1:]
    return drawn.at[tuple(index_at)].set(low).at[tuple(next_to)].set(high)


def levels(rng, dims, shards, low, high):
    factor_of = 1.0
    for axis_at, parts in shards:
        heights = jax.random.uniform(jax.random.fold_in(jax.random.fold_in(rng, 6), axis_at), (parts,), jnp.float32, low / len(shards), high / len(shards))
        factor_of = factor_of * jnp.repeat(jnp.exp(heights), dims[axis_at] // parts).reshape((-1,) + (1,) * (len(dims) - 1 - axis_at))
    return factor_of


def centred(stream_key, extent, deviation, bound, cuts=(), kind=jnp.bfloat16):
    values = deviation * jax.random.normal(stream_key, extent, jnp.float32)
    if cuts:
        values = values * levels(stream_key, extent, cuts, -0.22, 0.18)
    return jnp.clip(values, -bound, bound).astype(kind)


def setup_inputs(seed: int = 0, part: int = 0) -> dict:
    keys = jax.random.split(jax.random.key(seed), 8)
    part_keys = jax.random.split(jax.random.fold_in(keys[7], part), 8)
    return {
        "psi": centred(part_keys[0], (HR * N_TASK, NV * MR), 1.0, 6.0, ((0, 16),)),
        "left_env": centred(part_keys[1], (N_OPS, N_TASK, TPO, SMAX, SMAX), SMAX ** -0.5, 0.375, ((0, 4), (1, 4))),
        "right_env": centred(part_keys[2], (N_OPS, TERMS, MR, MR), (MR * TERMS * N_OPS) ** -0.5, 0.09375, ((0, 4),)),
        "sec_tiles": draw_sec_tiles(jax.random.fold_in(jax.random.fold_in(keys[7], part), 71), part),
        "task_sector": draw_task_sector(jax.random.fold_in(jax.random.fold_in(keys[7], part), 71), part),
        "task_term": draw_task_term(jax.random.fold_in(jax.random.fold_in(keys[7], part), 71), part),
        "task_live": set_ends((jax.random.randint(part_keys[6], (N_OPS, N_TASK, TPO), 0, 3) < 2).astype(jnp.int32), jax.random.fold_in(part_keys[6], 1), 0, 1),
    }


def reference(psi, left_env, right_env, sec_tiles, task_sector, task_term, task_live):
    columns = NV * MR
    sector_rows = sec_tiles * TILE
    starts = jnp.cumsum(sector_rows, axis=1) - sector_rows
    home_blocks = psi.reshape(N_TASK, HR, columns)
    padded = jnp.concatenate([home_blocks, jnp.zeros((N_TASK, SMAX, columns), psi.dtype)], axis=1)
    slot_home = (jnp.arange(TPO) % N_TASK).astype(jnp.int32)
    offsets = jnp.arange(SMAX).astype(jnp.int32)
    right_blocks = right_env.astype(jnp.float32)
    groups = jnp.arange(N_OPS).astype(jnp.int32)

    def owner_step(placed, owner_id):
        sector = task_sector[owner_id]
        row_count = sector_rows[slot_home, sector]
        row_start = starts[slot_home, sector]
        keep_rows = offsets[None, :] < row_count[:, None]
        row_ids = (row_start[:, None] + offsets[None, :]).astype(jnp.int32)
        pieces = padded[slot_home[:, None], row_ids].astype(jnp.float32)
        pieces = jnp.where(keep_rows[:, :, None], pieces, jnp.float32(0.0))
        left_blocks = left_env[:, owner_id].astype(jnp.float32)
        mixed_rows = jnp.einsum('gkrs,ksc->gkrc', left_blocks, pieces, precision=lax.Precision.HIGHEST)
        mixed_rows = jnp.where(keep_rows[None, :, :, None], mixed_rows, jnp.float32(0.0))
        mixed_rows = lax.optimization_barrier(mixed_rows.astype(jnp.bfloat16)).astype(jnp.float32)
        mixed_rows = mixed_rows.reshape(N_OPS, TPO, SMAX, NV, MR)
        chosen = right_blocks[groups[:, None], task_term[owner_id][None, :]]
        result = jnp.einsum('gkrvm,gkmn->gkrvn', mixed_rows, chosen, precision=lax.Precision.HIGHEST)
        result = result * task_live[:, owner_id].astype(jnp.float32)[:, :, None, None, None]
        result = lax.optimization_barrier(result.astype(jnp.bfloat16)).astype(jnp.float32)
        summed = jnp.sum(result, axis=0).reshape(TPO, SMAX, columns)
        placed = placed.at[slot_home[:, None], row_ids].add(summed)
        return placed, None

    start_value = jnp.zeros((N_TASK, HR + SMAX, columns), jnp.float32)
    placed, _ = lax.scan(owner_step, start_value, jnp.arange(N_TASK).astype(jnp.int32))
    return placed[:, :HR].reshape(N_TASK * HR, columns).astype(jnp.bfloat16)
```

```python
import functools

import jax
import jax.numpy as jnp
from jax import lax
from jax.experimental import pallas as pl
from jax.experimental.pallas import tpu as pltpu
from jax.sharding import PartitionSpec as P

TILE = 128
MR = 128
NV = 3


def lookup(entries, selected):
    sector_marks = selected[..., None] == jnp.arange(entries.shape[-1])
    return jnp.sum(jnp.where(sector_marks, entries, 0), axis=-1)


def apply_terms(blocks, pieces, pattern, keep_rows, term_ids, live_flags, right_blocks):
    mixed_rows = jnp.einsum(pattern, blocks, pieces, preferred_element_type=jnp.float32)
    mixed_rows = jnp.where(keep_rows[..., None], mixed_rows, 0.0).astype(jnp.bfloat16)
    leading = mixed_rows.shape[:3]
    per_vector = mixed_rows.reshape(leading + (NV, MR))
    chosen = right_blocks[term_ids]
    result = jnp.einsum("abrvm,abmn->abrvn", per_vector, chosen, preferred_element_type=jnp.float32)
    result = result * live_flags[:, :, None, None, None].astype(jnp.float32)
    return result.reshape(leading + (NV * MR,)).astype(jnp.bfloat16)


def body(psi, left_env, right_env, sec_tiles, task_sector, task_term, task_live):
    owners = lax.axis_size("task")
    owner_index = lax.axis_index("task")
    columns = psi.shape[1]
    span_rows = left_env.shape[-1]
    slot_count = task_sector.shape[1]
    pair_count = slot_count // owners
    sector_count = sec_tiles.shape[1]
    own_block = lax.all_gather(psi, "ops", axis=0, tiled=True)
    own_rows = own_block.shape[0]
    sector_rows = lax.dynamic_index_in_dim(sec_tiles, owner_index, 0, keepdims=False) * TILE
    starts = jnp.cumsum(sector_rows) - sector_rows
    padded = jnp.concatenate([own_block, jnp.zeros((span_rows, columns), own_block.dtype)], axis=0)
    offsets = jnp.arange(span_rows)
    sent_sector = lax.dynamic_index_in_dim(
        task_sector.reshape(owners, pair_count, owners), owner_index, 2, keepdims=False
    )
    counts = lookup(sector_rows, sent_sector)
    begins = lookup(starts, sent_sector)
    send_keep = offsets < counts[..., None]
    row_ids = begins[..., None] + offsets
    pieces = jnp.where(send_keep[..., None], padded[row_ids], jnp.zeros((), own_block.dtype))
    group_live = task_live[0]
    right_blocks = right_env[0]
    arrived = lax.all_to_all(pieces, "task", split_axis=0, concat_axis=0, tiled=True)
    my_sectors = lax.dynamic_index_in_dim(task_sector, owner_index, 0, keepdims=False).reshape(
        pair_count, owners
    )
    all_rows = sec_tiles * TILE
    slot_rows = lookup(all_rows[None, :, :], my_sectors)
    own_keep = offsets < slot_rows[..., None]
    term_ids = lax.dynamic_index_in_dim(task_term, owner_index, 0, keepdims=False).reshape(
        pair_count, owners
    )
    live_flags = lax.dynamic_index_in_dim(group_live, owner_index, 0, keepdims=False).reshape(
        pair_count, owners
    )
    blocks = left_env.reshape(pair_count, owners, span_rows, span_rows)
    result = apply_terms(
        blocks, arrived, "tirs,itsc->tirc", own_keep, term_ids, live_flags, right_blocks
    )
    returned = lax.all_to_all(result, "task", split_axis=1, concat_axis=1, tiled=True)
    sum_pattern = "jtl,tjrc->lrc"
    sector_marks = (sent_sector[..., None] == jnp.arange(sector_count)).astype(jnp.bfloat16)
    sector_sums = jnp.einsum(
        sum_pattern, sector_marks, returned, preferred_element_type=jnp.float32
    )
    placed = jnp.zeros((own_rows + span_rows, columns), jnp.float32)
    for sector in range(sector_count):
        placed = lax.dynamic_update_slice_in_dim(placed, sector_sums[sector], starts[sector], 0)
    summed = lax.psum_scatter(placed[:own_rows], "ops", scatter_dimension=0, tiled=True)
    return summed.astype(jnp.bfloat16)


MESH = pl.DeviceIdType.MESH
VMEM_LIMIT = 32 * 1024 * 1024


def place():
    z = lax.axis_index("task")
    o = lax.axis_index("ops")
    across = lax.rem(o + 2, 4)
    sibling = o + 1 - 2 * lax.rem(o, 2)
    return z, o, across, sibling


def enter(z, across, sibling, depth):
    barrier = pltpu.get_barrier_semaphore()

    def greet(**where):
        pl.semaphore_signal(barrier, inc=1, device_id=where, device_id_type=MESH)

    greet(ops=across)
    greet(ops=sibling)

    @pl.when(z > 0)
    def _():
        greet(task=z - 1)

    @pl.when(z < depth - 1)
    def _():
        greet(task=z + 1)

    inner = jnp.where(z > 0, 1, 0) + jnp.where(z < depth - 1, 1, 0)
    pl.semaphore_wait(barrier, 2 + inner)


def gather_kernel(depth, psi_ref, out_ref, send_sem, recv_sem, own_sem):
    z, o, across, sibling = place()
    enter(z, across, sibling, depth)
    up, down, side, core = 0, 1, 2, 3

    def copy(way, at, col, own=False):
        block = at * 4 + col
        where = ({"task": z + 1}, {"task": z - 1}, {"ops": across}, {"ops": sibling})[way]
        return pltpu.make_async_remote_copy(
            src_ref=psi_ref if own else out_ref.at[block],
            dst_ref=out_ref.at[block],
            send_sem=send_sem.at[way, block],
            recv_sem=recv_sem.at[block],
            device_id=where,
            device_id_type=MESH,
        )

    def arrived(at, col):
        copy(side, at, col).wait_recv()

    def offsets(t):
        return ((-t, z - t >= 0), (t, z + t <= depth - 1))

    @pl.when(z < depth - 1)
    def _():
        copy(up, z, o, True).start()

    @pl.when(z > 0)
    def _():
        copy(down, z, o, True).start()

    copy(side, z, o, True).start()
    copy(core, z, o, True).start()
    keep = pltpu.make_async_copy(psi_ref, out_ref.at[z * 4 + o], own_sem)
    keep.start()

    for t in range(1, depth):
        for step, there in offsets(t):
            at = z + step

            @pl.when(there)
            def _():
                arrived(at, o)

                if step < 0:
                    @pl.when(z < depth - 1)
                    def _():
                        copy(up, at, o).start()
                else:
                    @pl.when(z > 0)
                    def _():
                        copy(down, at, o).start()

                copy(side, at, o).start()
                copy(core, at, o).start()
        if t == 1:
            arrived(z, across)
            copy(core, z, across).start()
        else:
            for step, there in offsets(t - 1):
                at = z + step

                @pl.when(there)
                def _():
                    arrived(at, across)
                    copy(core, at, across).start()
    for step, there in offsets(depth - 1):
        at = z + step

        @pl.when(there)
        def _():
            arrived(at, across)
            copy(core, at, across).start()

    other = lax.rem(sibling + 2, 4)
    for at in range(depth):
        arrived(at, sibling)
        arrived(at, other)
        copy(side, at, o).wait_send()
        copy(core, at, o).wait_send()
        copy(core, at, across).wait_send()

        @pl.when((z < depth - 1) & (at <= z))
        def _():
            copy(up, at, o).wait_send()

        @pl.when((z > 0) & (at >= z))
        def _():
            copy(down, at, o).wait_send()
    keep.wait()


def gather(psi, depth):
    return pl.pallas_call(
        functools.partial(gather_kernel, depth),
        out_shape=jax.ShapeDtypeStruct((depth * 4,) + psi.shape, psi.dtype),
        in_specs=[pl.BlockSpec(memory_space=pltpu.VMEM)],
        out_specs=pl.BlockSpec(memory_space=pltpu.VMEM),
        scratch_shapes=[
            pltpu.SemaphoreType.DMA((4, depth * 4)),
            pltpu.SemaphoreType.DMA((depth * 4,)),
            pltpu.SemaphoreType.DMA,
        ],
        compiler_params=pltpu.CompilerParams(
            collective_id=0, has_side_effects=True, vmem_limit_bytes=VMEM_LIMIT
        ),
    )(psi)


def scatter_kernel(depth, part_ref, out_ref, core_buf, side_buf, up_buf, down_buf, side_out, z_out,
                   core_send, side_send, z_send, core_recv, side_recv, up_recv, down_recv):
    z, o, across, sibling = place()
    enter(z, across, sibling, depth)
    other = lax.rem(sibling + 2, 4)

    def core_copy(at, far):
        return pltpu.make_async_remote_copy(
            src_ref=part_ref.at[at * 4 + (other if far else sibling)],
            dst_ref=core_buf.at[int(far), at],
            send_sem=core_send.at[int(far), at],
            recv_sem=core_recv.at[int(far), at],
            device_id={"ops": sibling},
            device_id_type=MESH,
        )

    def side_copy(at):
        return pltpu.make_async_remote_copy(
            src_ref=side_out.at[at],
            dst_ref=side_buf.at[at],
            send_sem=side_send.at[at],
            recv_sem=side_recv.at[at],
            device_id={"ops": across},
            device_id_type=MESH,
        )

    def z_copy(at, rising):
        return pltpu.make_async_remote_copy(
            src_ref=z_out.at[at],
            dst_ref=(up_buf if rising else down_buf).at[at],
            send_sem=z_send.at[at],
            recv_sem=(up_recv if rising else down_recv).at[at],
            device_id={"task": z + 1 if rising else z - 1},
            device_id_type=MESH,
        )

    def wide(value):
        return value.astype(jnp.float32)

    order = []
    for t in range(depth - 1, 0, -1):
        order += [(t, z + t <= depth - 1), (-t, z - t >= 0)]
    order.append((0, None))

    def each(work):
        for step, there in order:
            if there is None:
                work(z, step)
            else:
                pl.when(there)(functools.partial(work, z + step, step))

    def send_core_far(at, step):
        core_copy(at, True).start()

    def send_core_near(at, step):
        core_copy(at, False).start()

    def send_side(at, step):
        core_copy(at, True).wait_recv()
        side_out[at] = (wide(part_ref[at * 4 + across]) + wide(core_buf[1, at])).astype(jnp.bfloat16)
        side_copy(at).start()

    def gathered(at):
        core_copy(at, False).wait_recv()
        side_copy(at).wait_recv()
        return wide(part_ref[at * 4 + o]) + wide(core_buf[0, at]) + wide(side_buf[at])

    def send_z(at, step):
        if step == 0:
            return
        rising = step > 0
        buf = up_buf if rising else down_buf
        first = (z == 0) if rising else (z == depth - 1)

        @pl.when(first)
        def _():
            z_out[at] = gathered(at).astype(jnp.bfloat16)

        @pl.when(jnp.logical_not(first))
        def _():
            total = gathered(at)
            z_copy(at, rising).wait_recv()
            z_out[at] = (total + wide(buf[at])).astype(jnp.bfloat16)

        z_copy(at, rising).start()

    each(send_core_far)
    each(send_core_near)
    each(send_side)
    each(send_z)

    @pl.when(z == 0)
    def _():
        total = gathered(z)
        z_copy(z, False).wait_recv()
        out_ref[...] = (total + wide(down_buf[z])).astype(jnp.bfloat16)

    @pl.when(z == depth - 1)
    def _():
        total = gathered(z)
        z_copy(z, True).wait_recv()
        out_ref[...] = (total + wide(up_buf[z])).astype(jnp.bfloat16)

    @pl.when((z > 0) & (z < depth - 1))
    def _():
        total = gathered(z)
        z_copy(z, True).wait_recv()
        z_copy(z, False).wait_recv()
        out_ref[...] = (total + wide(up_buf[z]) + wide(down_buf[z])).astype(jnp.bfloat16)

    def finish(at, step):
        core_copy(at, True).wait_send()
        core_copy(at, False).wait_send()
        side_copy(at).wait_send()
        if step != 0:
            z_copy(at, step > 0).wait_send()

    each(finish)


def scatter(partial, depth):
    block = partial.shape[1:]
    dma = pltpu.SemaphoreType.DMA
    slots = pltpu.VMEM((depth,) + block, jnp.bfloat16)
    return pl.pallas_call(
        functools.partial(scatter_kernel, depth),
        out_shape=jax.ShapeDtypeStruct(block, jnp.bfloat16),
        in_specs=[pl.BlockSpec(memory_space=pltpu.VMEM)],
        out_specs=pl.BlockSpec(memory_space=pltpu.VMEM),
        scratch_shapes=[pltpu.VMEM((2, depth) + block, jnp.bfloat16)] + [slots] * 5 + [
            dma((2, depth)), dma((depth,)), dma((depth,)),
            dma((2, depth)), dma((depth,)), dma((depth,)), dma((depth,)),
        ],
        compiler_params=pltpu.CompilerParams(
            collective_id=1, has_side_effects=True, vmem_limit_bytes=VMEM_LIMIT
        ),
    )(partial)


def apply_kernel(pairs, owners, table_ref, psi_ref, env_ref, right_ref, out_ref, acc):
    home = pl.program_id(0)
    acc[...] = jnp.zeros_like(acc)
    for pair in range(pairs):
        slot = pair * owners + home
        start = pl.multiple_of(table_ref[0, slot], TILE)
        tiles = table_ref[1, slot]
        term = table_ref[2, slot]
        live = table_ref[3, slot]

        def run(count):
            rows = count * TILE
            mixed = jnp.dot(
                env_ref[pair, 0, :rows, :rows],
                psi_ref[pl.ds(start, rows), :],
                preferred_element_type=jnp.float32,
            ).astype(jnp.bfloat16)
            right = right_ref[term]
            for v in range(NV):
                cols = slice(v * MR, (v + 1) * MR)
                acc[pl.ds(start, rows), cols] += jnp.dot(
                    mixed[:, cols], right, preferred_element_type=jnp.float32
                )

        for count in (1, 2):
            pl.when((live != 0) & (tiles == count))(functools.partial(run, count))
    out_ref[...] = acc[...].astype(jnp.bfloat16)


def apply_slots(table, psi, env, right):
    pairs, owners, span = env.shape[:3]
    own, columns = psi.shape[0] // owners, psi.shape[1]
    return pl.pallas_call(
        functools.partial(apply_kernel, pairs, owners),
        out_shape=jax.ShapeDtypeStruct(psi.shape, jnp.bfloat16),
        grid_spec=pltpu.PrefetchScalarGridSpec(
            num_scalar_prefetch=1,
            grid=(owners,),
            in_specs=[
                pl.BlockSpec((own, columns), lambda i, table: (i, 0)),
                pl.BlockSpec((pairs, 1, span, span), lambda i, table: (0, i, 0, 0)),
                pl.BlockSpec(right.shape, lambda i, table: (0, 0, 0)),
            ],
            out_specs=pl.BlockSpec((own, columns), lambda i, table: (i, 0)),
            scratch_shapes=[pltpu.VMEM((own, columns), jnp.float32)],
        ),
        compiler_params=pltpu.CompilerParams(vmem_limit_bytes=VMEM_LIMIT),
    )(table, psi, env, right)


def slot_table(sec_tiles, task_sector, task_term, task_live):
    owners = sec_tiles.shape[0]
    me = lax.axis_index("task")
    mine = lambda a: lax.dynamic_index_in_dim(a, me, 0, keepdims=False)
    sectors = mine(task_sector)
    home = jnp.arange(sectors.shape[0]) % owners
    marks = sectors[:, None] == jnp.arange(sec_tiles.shape[1])
    starts = jnp.cumsum(sec_tiles, axis=1) - sec_tiles
    pick = lambda a: jnp.sum(jnp.where(marks, a[home], 0), axis=1)
    return jnp.stack([pick(starts) * TILE, pick(sec_tiles), mine(task_term), mine(task_live[0])]).astype(jnp.int32)


def small_body(psi, left_env, right_env, sec_tiles, task_sector, task_term, task_live):
    depth = lax.axis_size("task")
    span = left_env.shape[-1]
    table = slot_table(sec_tiles, task_sector, task_term, task_live)
    whole = gather(psi, depth).reshape(-1, psi.shape[1])
    env = left_env.reshape(-1, depth, span, span)
    partial = apply_slots(table, whole, env, right_env[0])
    return scatter(partial.reshape((-1,) + psi.shape), depth)


def solution(mesh):
    paired = mesh.shape["ops"] == 4 and mesh.shape["task"] <= 4
    return jax.shard_map(
        small_body if paired else body,
        mesh=mesh,
        in_specs=(
            P(("copies", "task", "ops"), None),
            P(("copies", "ops"), "task", None, None, None),
            P(("copies", "ops"), None, None, None),
            P("copies", None),
            P("copies", None),
            P("copies", None),
            P(("copies", "ops"), None, None),
        ),
        out_specs=P(("copies", "task", "ops"), None),
        check_vma=False,
    )
```

```python
import functools
import math

import jax
import jax.numpy as jnp
from jax import lax
from jax.experimental import pallas as pl
from jax.experimental.pallas import tpu as pltpu
from jax.sharding import PartitionSpec as P

TILE = 128
MR = 128
NV = 3


def lookup(entries, selected):
    sector_marks = selected[..., None] == jnp.arange(entries.shape[-1])
    return jnp.sum(jnp.where(sector_marks, entries, 0), axis=-1)


def apply_terms(blocks, pieces, pattern, keep_rows, term_ids, live_flags, right_blocks):
    mixed_rows = jnp.einsum(pattern, blocks, pieces, preferred_element_type=jnp.float32)
    mixed_rows = jnp.where(keep_rows[..., None], mixed_rows, 0.0).astype(jnp.bfloat16)
    leading = mixed_rows.shape[:3]
    per_vector = mixed_rows.reshape(leading + (NV, MR))
    chosen = right_blocks[term_ids]
    result = jnp.einsum("abrvm,abmn->abrvn", per_vector, chosen, preferred_element_type=jnp.float32)
    result = result * live_flags[:, :, None, None, None].astype(jnp.float32)
    return result.reshape(leading + (NV * MR,)).astype(jnp.bfloat16)


def body(psi, left_env, right_env, sec_tiles, task_sector, task_term, task_live):
    owners = lax.axis_size("task")
    owner_index = lax.axis_index("task")
    columns = psi.shape[1]
    span_rows = left_env.shape[-1]
    slot_count = task_sector.shape[1]
    pair_count = slot_count // owners
    sector_count = sec_tiles.shape[1]
    own_block = lax.all_gather(psi, "ops", axis=0, tiled=True)
    own_rows = own_block.shape[0]
    sector_rows = lax.dynamic_index_in_dim(sec_tiles, owner_index, 0, keepdims=False) * TILE
    starts = jnp.cumsum(sector_rows) - sector_rows
    padded = jnp.concatenate([own_block, jnp.zeros((span_rows, columns), own_block.dtype)], axis=0)
    offsets = jnp.arange(span_rows)
    sent_sector = lax.dynamic_index_in_dim(
        task_sector.reshape(owners, pair_count, owners), owner_index, 2, keepdims=False
    )
    counts = lookup(sector_rows, sent_sector)
    begins = lookup(starts, sent_sector)
    send_keep = offsets < counts[..., None]
    row_ids = begins[..., None] + offsets
    pieces = jnp.where(send_keep[..., None], padded[row_ids], jnp.zeros((), own_block.dtype))
    group_live = task_live[0]
    right_blocks = right_env[0]
    arrived = lax.all_to_all(pieces, "task", split_axis=0, concat_axis=0, tiled=True)
    my_sectors = lax.dynamic_index_in_dim(task_sector, owner_index, 0, keepdims=False).reshape(
        pair_count, owners
    )
    all_rows = sec_tiles * TILE
    slot_rows = lookup(all_rows[None, :, :], my_sectors)
    own_keep = offsets < slot_rows[..., None]
    term_ids = lax.dynamic_index_in_dim(task_term, owner_index, 0, keepdims=False).reshape(
        pair_count, owners
    )
    live_flags = lax.dynamic_index_in_dim(group_live, owner_index, 0, keepdims=False).reshape(
        pair_count, owners
    )
    blocks = left_env.reshape(pair_count, owners, span_rows, span_rows)
    result = apply_terms(
        blocks, arrived, "tirs,itsc->tirc", own_keep, term_ids, live_flags, right_blocks
    )
    returned = lax.all_to_all(result, "task", split_axis=1, concat_axis=1, tiled=True)
    sum_pattern = "jtl,tjrc->lrc"
    sector_marks = (sent_sector[..., None] == jnp.arange(sector_count)).astype(jnp.bfloat16)
    sector_sums = jnp.einsum(
        sum_pattern, sector_marks, returned, preferred_element_type=jnp.float32
    )
    placed = jnp.zeros((own_rows + span_rows, columns), jnp.float32)
    for sector in range(sector_count):
        placed = lax.dynamic_update_slice_in_dim(placed, sector_sums[sector], starts[sector], 0)
    summed = lax.psum_scatter(placed[:own_rows], "ops", scatter_dimension=0, tiled=True)
    return summed.astype(jnp.bfloat16)


MESH = pl.DeviceIdType.MESH
VMEM_LIMIT = 32 * 1024 * 1024


def place():
    z = lax.axis_index("task")
    o = lax.axis_index("ops")
    across = lax.rem(o + 2, 4)
    sibling = o + 1 - 2 * lax.rem(o, 2)
    return z, o, across, sibling


def enter(z, across, sibling, depth):
    barrier = pltpu.get_barrier_semaphore()

    def greet(**where):
        pl.semaphore_signal(barrier, inc=1, device_id=where, device_id_type=MESH)

    greet(ops=across)
    greet(ops=sibling)

    @pl.when(z > 0)
    def _():
        greet(task=z - 1)

    @pl.when(z < depth - 1)
    def _():
        greet(task=z + 1)

    inner = jnp.where(z > 0, 1, 0) + jnp.where(z < depth - 1, 1, 0)
    pl.semaphore_wait(barrier, 2 + inner)


def whole_kernel(depth, psi_ref, env_ref, right_ref, tiles_ref, sector_ref, term_ref, live_ref, out_ref, *scratch):
    steps = 2 * depth - 1
    homes, scratch = scratch[:steps], scratch[steps:]
    (env, right, tiles, sector, term, live, first_tile, end_tile, mixed, part, core_buf, side_buf, up_buf, down_buf,
     side_out, z_out, send_sem, recv_sem, local_sem, core_send, side_send, z_send,
     core_recv, side_recv, up_recv, down_recv) = scratch
    z, o, across, sibling = place()
    other = lax.rem(sibling + 2, 4)
    pairs = env.shape[0]
    units, unit = psi_ref.shape[:2]
    rows = units * unit
    per_tile = TILE // unit
    own_tiles = homes[0].shape[0] // per_tile
    sectors = tiles.shape[1]
    up, down, side, core = 0, 1, 2, 3

    def block(step, col):
        return homes[step + depth - 1].at[pl.ds(col * units, units)]

    loads = [
        pltpu.make_async_copy(source, target, local_sem.at[i])
        for i, (source, target) in enumerate((
            (psi_ref, block(0, o)), (tiles_ref, tiles), (sector_ref, sector), (term_ref, term), (live_ref, live),
            (right_ref, right), (env_ref, env),
        ))
    ]
    for load in loads:
        load.start()
    enter(z, across, sibling, depth)

    def copy(way, step, col):
        shift = (-1, 1, 0, 0)[way]
        where = ({"task": z + 1}, {"task": z - 1}, {"ops": across}, {"ops": sibling})[way]
        index = (z + step) * 4 + col
        own = step == 0 and col is o
        return pltpu.make_async_remote_copy(
            src_ref=psi_ref if own else block(step, col),
            dst_ref=block(step + shift, col),
            send_sem=send_sem.at[way, index],
            recv_sem=recv_sem.at[index],
            device_id=where,
            device_id_type=MESH,
        )

    def arrived(step, col):
        copy(core, step, col).wait_recv()

    def offsets(t):
        return ((-t, z - t >= 0), (t, z + t <= depth - 1))

    def core_copy(at, far):
        col = other if far else sibling
        return pltpu.make_async_remote_copy(
            src_ref=part.at[at, pl.ds(pl.multiple_of(col * rows, 16), rows)],
            dst_ref=core_buf.at[int(far), at],
            send_sem=core_send.at[int(far), at],
            recv_sem=core_recv.at[int(far), at],
            device_id={"ops": sibling},
            device_id_type=MESH,
        )

    def side_copy(at):
        return pltpu.make_async_remote_copy(
            src_ref=side_out.at[at],
            dst_ref=side_buf.at[at],
            send_sem=side_send.at[at],
            recv_sem=side_recv.at[at],
            device_id={"ops": across},
            device_id_type=MESH,
        )

    def z_copy(at, rising):
        return pltpu.make_async_remote_copy(
            src_ref=z_out.at[at],
            dst_ref=(up_buf if rising else down_buf).at[at],
            send_sem=z_send.at[at],
            recv_sem=(up_recv if rising else down_recv).at[at],
            device_id={"task": z + 1 if rising else z - 1},
            device_id_type=MESH,
        )

    def wide(value):
        return value.astype(jnp.float32)

    def part_rows(at, col):
        return wide(part[at, pl.ds(pl.multiple_of(col * rows, 16), rows), :])

    def apply_home(step):
        home = z + step
        held = homes[step + depth - 1]

        def one_slot(pair, _):
            slot = pair * depth + home
            which = sector[z, slot]
            start = jnp.int32(0)
            for earlier in range(sectors - 1):
                start += jnp.where(earlier < which, tiles[home, earlier], 0)
            count = tiles[home, which]
            first_tile[pair] = start
            end_tile[pair] = jnp.where(live[0, z, slot] != 0, start + count, start)
            next_tile = jnp.minimum(start + 1, own_tiles - 1)
            pieces = [held[start * per_tile + i] for i in range(per_tile)]
            for i in range(per_tile):
                piece = held[next_tile * per_tile + i]
                pieces.append(jnp.where(count > 1, piece, jnp.zeros_like(piece)))
            rows_in = jnp.concatenate(pieces, axis=0)
            turned = jnp.dot(env[pair, home], rows_in, preferred_element_type=jnp.float32).astype(jnp.bfloat16)
            chosen = right[term[z, slot]]
            for v in range(NV):
                cols = slice(v * MR, (v + 1) * MR)
                result = jnp.dot(
                    turned[:, cols], chosen, preferred_element_type=jnp.float32
                ).astype(jnp.bfloat16)
                mixed[pair, 0, :, cols] = result[:TILE]
                mixed[pair, 1, :, cols] = result[TILE:]
            return 0

        lax.fori_loop(0, pairs, one_slot, 0, unroll=UNROLL)

        def one_tile(tile, _):
            for v in range(NV):
                cols = slice(v * MR, (v + 1) * MR)
                total = jnp.zeros((TILE, MR), jnp.float32)
                for pair in range(pairs):
                    start, end = first_tile[pair], end_tile[pair]
                    weight = jnp.where((tile >= start) & (tile < end), 1.0, 0.0)
                    offset = jnp.where(tile > start, 1, 0)
                    total += weight * wide(mixed[pair, offset, :, cols])
                part[home, pl.ds(pl.multiple_of(tile * TILE, TILE), TILE), cols] = total.astype(jnp.bfloat16)
            return 0

        lax.fori_loop(0, own_tiles, one_tile, 0)
        core_copy(home, True).start()
        core_copy(home, False).start()

    def finish_home(step):
        arrived(step, across)
        copy(core, step, across).start()
        arrived(step, sibling)
        arrived(step, other)
        apply_home(step)

    def send_side(at):
        core_copy(at, True).wait_recv()
        side_out[at] = (part_rows(at, across) + wide(core_buf[1, at])).astype(jnp.bfloat16)
        side_copy(at).start()

    def gathered(at):
        core_copy(at, False).wait_recv()
        side_copy(at).wait_recv()
        return part_rows(at, o) + wide(core_buf[0, at]) + wide(side_buf[at])

    def send_z(step):
        at = z + step
        rising = step > 0
        buf = up_buf if rising else down_buf
        first = (z == 0) if rising else (z == depth - 1)

        @pl.when(first)
        def _():
            z_out[at] = gathered(at).astype(jnp.bfloat16)

        @pl.when(jnp.logical_not(first))
        def _():
            total = gathered(at)
            z_copy(at, rising).wait_recv()
            z_out[at] = (total + wide(buf[at])).astype(jnp.bfloat16)

        z_copy(at, rising).start()

    @pl.when(z < depth - 1)
    def _():
        copy(up, 0, o).start()

    @pl.when(z > 0)
    def _():
        copy(down, 0, o).start()

    copy(side, 0, o).start()
    copy(core, 0, o).start()

    def forward(t):
        for step, there in offsets(t):
            @pl.when(there)
            def _():
                arrived(step, o)

                if 1 - depth < step < 0:
                    @pl.when(z < depth - 1)
                    def _():
                        copy(up, step, o).start()
                if 0 < step < depth - 1:
                    @pl.when(z > 0)
                    def _():
                        copy(down, step, o).start()

                copy(side, step, o).start()
                copy(core, step, o).start()

    forward(1)
    for load in loads:
        load.wait()
    finish_home(0)
    for t in range(1, depth):
        if t + 1 < depth:
            forward(t + 1)
        if t + 1 == depth - 1:
            send_side(z)
        for step, there in offsets(t):
            pl.when(there)(functools.partial(finish_home, step))
    if depth < 3:
        send_side(z)

    order = []
    for t in range(depth - 1, 0, -1):
        order += offsets(t)[::-1]
    for step, there in order:
        pl.when(there)(functools.partial(send_side, z + step))
    for step, there in order:
        pl.when(there)(functools.partial(send_z, step))

    total = gathered(z)

    @pl.when(z == 0)
    def _():
        z_copy(z, False).wait_recv()
        out_ref[...] = (total + wide(down_buf[z])).astype(jnp.bfloat16)

    @pl.when(z == depth - 1)
    def _():
        z_copy(z, True).wait_recv()
        out_ref[...] = (total + wide(up_buf[z])).astype(jnp.bfloat16)

    @pl.when((z > 0) & (z < depth - 1))
    def _():
        z_copy(z, True).wait_recv()
        z_copy(z, False).wait_recv()
        out_ref[...] = (total + wide(up_buf[z]) + wide(down_buf[z])).astype(jnp.bfloat16)

    def drain(step):
        at = z + step
        core_copy(at, True).wait_send()
        core_copy(at, False).wait_send()
        side_copy(at).wait_send()
        copy(side, step, o).wait_send()
        copy(core, step, o).wait_send()
        copy(core, step, across).wait_send()
        if step != 0:
            z_copy(at, step > 0).wait_send()
        if 1 - depth < step <= 0:
            @pl.when(z < depth - 1)
            def _():
                copy(up, step, o).wait_send()
        if 0 <= step < depth - 1:
            @pl.when(z > 0)
            def _():
                copy(down, step, o).wait_send()

    drain(0)
    for step, there in order:
        pl.when(there)(functools.partial(drain, step))


UNROLL = 2


def small_body(psi, left_env, right_env, sec_tiles, task_sector, task_term, task_live):
    depth = lax.axis_size("task")
    span = left_env.shape[-1]
    rows, columns = psi.shape
    env = left_env.reshape(-1, depth, span, span)
    right = right_env[0]
    pairs = env.shape[0]
    unit = math.gcd(rows, TILE)
    operands = (psi.reshape(-1, unit, columns), env, right, sec_tiles, task_sector, task_term, task_live)
    dma, vmem, smem = pltpu.SemaphoreType.DMA, pltpu.VMEM, pltpu.SMEM
    blocks = vmem((depth, rows, columns), jnp.bfloat16)
    ints = [smem(a.shape, jnp.int32) for a in operands[3:]]
    return pl.pallas_call(
        functools.partial(whole_kernel, depth),
        out_shape=jax.ShapeDtypeStruct(psi.shape, jnp.bfloat16),
        in_specs=[pl.BlockSpec(memory_space=pltpu.HBM)] * len(operands),
        out_specs=pl.BlockSpec(memory_space=pltpu.VMEM),
        scratch_shapes=[vmem((4 * rows // unit, unit, columns), jnp.bfloat16)] * (2 * depth - 1)
        + [vmem(env.shape, env.dtype), vmem(right.shape, right.dtype)] + ints
        + [smem((pairs,), jnp.int32)] * 2
        + [vmem((pairs, span // TILE, TILE, columns), jnp.bfloat16), vmem((depth, 4 * rows, columns), jnp.bfloat16),
           vmem((2, depth, rows, columns), jnp.bfloat16)] + [blocks] * 5
        + [dma((4, depth * 4)), dma((depth * 4,)), dma((len(operands),)), dma((2, depth)), dma((depth,)),
           dma((depth,)), dma((2, depth)), dma((depth,)), dma((depth,)), dma((depth,))],
        compiler_params=pltpu.CompilerParams(
            collective_id=0, has_side_effects=True, vmem_limit_bytes=VMEM_LIMIT
        ),
    )(*operands)


def solution(mesh):
    paired = mesh.shape["ops"] == 4 and mesh.shape["task"] <= 4
    return jax.shard_map(
        small_body if paired else body,
        mesh=mesh,
        in_specs=(
            P(("copies", "task", "ops"), None),
            P(("copies", "ops"), "task", None, None, None),
            P(("copies", "ops"), None, None, None),
            P("copies", None),
            P("copies", None),
            P("copies", None),
            P(("copies", "ops"), None, None),
        ),
        out_specs=P(("copies", "task", "ops"), None),
        check_vma=False,
    )
```

```python
import functools
import math

import jax
import jax.numpy as jnp
from jax import lax
from jax.experimental import pallas as pl
from jax.experimental.pallas import tpu as pltpu
from jax.sharding import PartitionSpec as P

TILE = 128
MR = 128
NV = 3


def lookup(entries, selected):
    sector_marks = selected[..., None] == jnp.arange(entries.shape[-1])
    return jnp.sum(jnp.where(sector_marks, entries, 0), axis=-1)


def apply_terms(blocks, pieces, pattern, keep_rows, term_ids, live_flags, right_blocks):
    mixed_rows = jnp.einsum(pattern, blocks, pieces, preferred_element_type=jnp.float32)
    mixed_rows = jnp.where(keep_rows[..., None], mixed_rows, 0.0).astype(jnp.bfloat16)
    leading = mixed_rows.shape[:3]
    per_vector = mixed_rows.reshape(leading + (NV, MR))
    chosen = right_blocks[term_ids]
    result = jnp.einsum("abrvm,abmn->abrvn", per_vector, chosen, preferred_element_type=jnp.float32)
    result = result * live_flags[:, :, None, None, None].astype(jnp.float32)
    return result.reshape(leading + (NV * MR,)).astype(jnp.bfloat16)


def body(psi, left_env, right_env, sec_tiles, task_sector, task_term, task_live):
    owners = lax.axis_size("task")
    owner_index = lax.axis_index("task")
    columns = psi.shape[1]
    span_rows = left_env.shape[-1]
    slot_count = task_sector.shape[1]
    pair_count = slot_count // owners
    sector_count = sec_tiles.shape[1]
    own_block = lax.all_gather(psi, "ops", axis=0, tiled=True)
    own_rows = own_block.shape[0]
    sector_rows = lax.dynamic_index_in_dim(sec_tiles, owner_index, 0, keepdims=False) * TILE
    starts = jnp.cumsum(sector_rows) - sector_rows
    padded = jnp.concatenate([own_block, jnp.zeros((span_rows, columns), own_block.dtype)], axis=0)
    offsets = jnp.arange(span_rows)
    sent_sector = lax.dynamic_index_in_dim(
        task_sector.reshape(owners, pair_count, owners), owner_index, 2, keepdims=False
    )
    counts = lookup(sector_rows, sent_sector)
    begins = lookup(starts, sent_sector)
    send_keep = offsets < counts[..., None]
    row_ids = begins[..., None] + offsets
    pieces = jnp.where(send_keep[..., None], padded[row_ids], jnp.zeros((), own_block.dtype))
    group_live = task_live[0]
    right_blocks = right_env[0]
    arrived = lax.all_to_all(pieces, "task", split_axis=0, concat_axis=0, tiled=True)
    my_sectors = lax.dynamic_index_in_dim(task_sector, owner_index, 0, keepdims=False).reshape(
        pair_count, owners
    )
    all_rows = sec_tiles * TILE
    slot_rows = lookup(all_rows[None, :, :], my_sectors)
    own_keep = offsets < slot_rows[..., None]
    term_ids = lax.dynamic_index_in_dim(task_term, owner_index, 0, keepdims=False).reshape(
        pair_count, owners
    )
    live_flags = lax.dynamic_index_in_dim(group_live, owner_index, 0, keepdims=False).reshape(
        pair_count, owners
    )
    blocks = left_env.reshape(pair_count, owners, span_rows, span_rows)
    result = apply_terms(
        blocks, arrived, "tirs,itsc->tirc", own_keep, term_ids, live_flags, right_blocks
    )
    returned = lax.all_to_all(result, "task", split_axis=1, concat_axis=1, tiled=True)
    sum_pattern = "jtl,tjrc->lrc"
    sector_marks = (sent_sector[..., None] == jnp.arange(sector_count)).astype(jnp.bfloat16)
    sector_sums = jnp.einsum(
        sum_pattern, sector_marks, returned, preferred_element_type=jnp.float32
    )
    placed = jnp.zeros((own_rows + span_rows, columns), jnp.float32)
    for sector in range(sector_count):
        placed = lax.dynamic_update_slice_in_dim(placed, sector_sums[sector], starts[sector], 0)
    summed = lax.psum_scatter(placed[:own_rows], "ops", scatter_dimension=0, tiled=True)
    return summed.astype(jnp.bfloat16)


MESH = pl.DeviceIdType.MESH
VMEM_LIMIT = 60 * 1024 * 1024


def place():
    z = lax.axis_index("task")
    o = lax.axis_index("ops")
    across = lax.rem(o + 2, 4)
    sibling = o + 1 - 2 * lax.rem(o, 2)
    return z, o, across, sibling


def enter(z, across, sibling, depth):
    barrier = pltpu.get_barrier_semaphore()

    def greet(**where):
        pl.semaphore_signal(barrier, inc=1, device_id=where, device_id_type=MESH)

    greet(ops=across)
    greet(ops=sibling)

    @pl.when(z > 0)
    def _():
        greet(task=z - 1)

    @pl.when(z < depth - 1)
    def _():
        greet(task=z + 1)

    inner = jnp.where(z > 0, 1, 0) + jnp.where(z < depth - 1, 1, 0)
    pl.semaphore_wait(barrier, 2 + inner)


def whole_kernel(depth, psi_ref, env_ref, right_ref, tiles_ref, sector_ref, term_ref, live_ref, out_ref, *scratch):
    steps = 2 * depth - 1
    homes, scratch = scratch[:steps], scratch[steps:]
    (env, right, tiles, sector, term, live, first_tile, end_tile, mixed, part, core_buf, side_buf, up_buf, down_buf,
     side_out, z_out, send_sem, recv_sem, local_sem, core_send, side_send, z_send,
     core_recv, side_recv, up_recv, down_recv) = scratch
    z, o, across, sibling = place()
    other = lax.rem(sibling + 2, 4)
    pairs = env.shape[0]
    units, unit = psi_ref.shape[:2]
    rows = units * unit
    per_tile = TILE // unit
    own_tiles = homes[0].shape[0] // per_tile
    sectors = tiles.shape[1]
    up, down, side, core = 0, 1, 2, 3

    def block(step, col):
        return homes[step + depth - 1].at[pl.ds(col * units, units)]

    loads = [
        pltpu.make_async_copy(source, target, local_sem.at[i])
        for i, (source, target) in enumerate((
            (psi_ref, block(0, o)), (tiles_ref, tiles), (sector_ref, sector), (term_ref, term), (live_ref, live),
            (right_ref, right), (env_ref, env),
        ))
    ]
    for load in loads:
        load.start()
    enter(z, across, sibling, depth)

    def copy(way, step, col):
        shift = (-1, 1, 0, 0)[way]
        where = ({"task": z + 1}, {"task": z - 1}, {"ops": across}, {"ops": sibling})[way]
        index = (z + step) * 4 + col
        own = step == 0 and col is o
        return pltpu.make_async_remote_copy(
            src_ref=psi_ref if own else block(step, col),
            dst_ref=block(step + shift, col),
            send_sem=send_sem.at[way, index],
            recv_sem=recv_sem.at[index],
            device_id=where,
            device_id_type=MESH,
        )

    def arrived(step, col):
        copy(core, step, col).wait_recv()

    def offsets(t):
        return ((-t, z - t >= 0), (t, z + t <= depth - 1))

    def core_copy(at, far):
        col = other if far else sibling
        return pltpu.make_async_remote_copy(
            src_ref=part.at[at, pl.ds(pl.multiple_of(col * rows, 16), rows)],
            dst_ref=core_buf.at[int(far), at],
            send_sem=core_send.at[int(far), at],
            recv_sem=core_recv.at[int(far), at],
            device_id={"ops": sibling},
            device_id_type=MESH,
        )

    def side_copy(at):
        return pltpu.make_async_remote_copy(
            src_ref=side_out.at[at],
            dst_ref=side_buf.at[at],
            send_sem=side_send.at[at],
            recv_sem=side_recv.at[at],
            device_id={"ops": across},
            device_id_type=MESH,
        )

    def z_copy(at, rising):
        return pltpu.make_async_remote_copy(
            src_ref=z_out.at[at],
            dst_ref=(up_buf if rising else down_buf).at[at],
            send_sem=z_send.at[at],
            recv_sem=(up_recv if rising else down_recv).at[at],
            device_id={"task": z + 1 if rising else z - 1},
            device_id_type=MESH,
        )

    def wide(value):
        return value.astype(jnp.float32)

    def part_rows(at, col):
        return wide(part[at, pl.ds(pl.multiple_of(col * rows, 16), rows), :])

    def apply_home(step):
        home = z + step
        held = homes[step + depth - 1]

        def one_slot(pair, _):
            slot = pair * depth + home
            which = sector[z, slot]
            start = jnp.int32(0)
            for earlier in range(sectors - 1):
                start += jnp.where(earlier < which, tiles[home, earlier], 0)
            count = tiles[home, which]
            first_tile[pair] = start
            end_tile[pair] = jnp.where(live[0, z, slot] != 0, start + count, start)
            next_tile = jnp.minimum(start + 1, own_tiles - 1)
            pieces = [held[start * per_tile + i] for i in range(per_tile)]
            for i in range(per_tile):
                piece = held[next_tile * per_tile + i]
                pieces.append(jnp.where(count > 1, piece, jnp.zeros_like(piece)))
            rows_in = jnp.concatenate(pieces, axis=0)
            turned = jnp.dot(env[pair, home], rows_in, preferred_element_type=jnp.float32).astype(jnp.bfloat16)
            chosen = right[term[z, slot]]
            for v in range(NV):
                cols = slice(v * MR, (v + 1) * MR)
                result = jnp.dot(
                    turned[:, cols], chosen, preferred_element_type=jnp.float32
                ).astype(jnp.bfloat16)
                mixed[pair, 0, :, cols] = result[:TILE]
                mixed[pair, 1, :, cols] = result[TILE:]
            return 0

        lax.fori_loop(0, pairs, one_slot, 0, unroll=UNROLL)

        def one_tile(tile, _):
            for v in range(NV):
                cols = slice(v * MR, (v + 1) * MR)
                total = jnp.zeros((TILE, MR), jnp.float32)
                for pair in range(pairs):
                    start, end = first_tile[pair], end_tile[pair]
                    weight = jnp.where((tile >= start) & (tile < end), 1.0, 0.0)
                    offset = jnp.where(tile > start, 1, 0)
                    total += weight * wide(mixed[pair, offset, :, cols])
                part[home, pl.ds(pl.multiple_of(tile * TILE, TILE), TILE), cols] = total.astype(jnp.bfloat16)
            return 0

        lax.fori_loop(0, own_tiles, one_tile, 0)
        core_copy(home, True).start()
        core_copy(home, False).start()

    def finish_home(step):
        arrived(step, across)
        copy(core, step, across).start()
        arrived(step, sibling)
        arrived(step, other)
        apply_home(step)

    def send_side(at, after=None):
        core_copy(at, True).wait_recv()
        side_out[at] = (part_rows(at, across) + wide(core_buf[1, at])).astype(jnp.bfloat16)
        if after is not None:
            side_copy(after).wait_send()
        side_copy(at).start()

    def gathered(at):
        core_copy(at, False).wait_recv()
        side_copy(at).wait_recv()
        return part_rows(at, o) + wide(core_buf[0, at]) + wide(side_buf[at])

    def send_z(step):
        at = z + step
        rising = step > 0
        buf = up_buf if rising else down_buf
        first = (z == 0) if rising else (z == depth - 1)

        @pl.when(first)
        def _():
            z_out[at] = gathered(at).astype(jnp.bfloat16)

        @pl.when(jnp.logical_not(first))
        def _():
            total = gathered(at)
            z_copy(at, rising).wait_recv()
            z_out[at] = (total + wide(buf[at])).astype(jnp.bfloat16)

        z_copy(at, rising).start()

    @pl.when(z < depth - 1)
    def _():
        copy(up, 0, o).start()

    @pl.when(z > 0)
    def _():
        copy(down, 0, o).start()

    copy(side, 0, o).start()
    copy(core, 0, o).start()

    def forward(t):
        for step, there in offsets(t):
            @pl.when(there)
            def _():
                arrived(step, o)

                if 1 - depth < step < 0:
                    @pl.when(z < depth - 1)
                    def _():
                        copy(up, step, o).start()
                if 0 < step < depth - 1:
                    @pl.when(z > 0)
                    def _():
                        copy(down, step, o).start()

                copy(side, step, o).start()
                copy(core, step, o).start()

    forward(1)
    for load in loads:
        load.wait()
    finish_home(0)
    for t in range(1, depth):
        if t + 1 < depth:
            forward(t + 1)
        if 2 * t >= depth - 1:
            @pl.when(jnp.maximum(z, depth - 1 - z) == t)
            def _():
                send_side(z)
        for step, there in offsets(t):
            pl.when(there)(functools.partial(finish_home, step))
    def send_back(steps_here):
        last = 0
        for i, step in enumerate(steps_here):
            send_side(z + step, z + last)
            last = step
            if i == 1:
                send_z(steps_here[0])
        side_copy(z + last).wait_send()
        for step in steps_here[1 if len(steps_here) > 1 else 0:]:
            send_z(step)

    order = []
    for t in range(depth - 1, 0, -1):
        order += offsets(t)[::-1]
    for at_z in range(depth):
        @pl.when(z == at_z)
        def _():
            steps_here = sorted((i - at_z for i in range(depth) if i != at_z), key=lambda i: (-abs(i), -i))
            send_back(steps_here)

    total = gathered(z)

    @pl.when(z == 0)
    def _():
        z_copy(z, False).wait_recv()
        out_ref[...] = (total + wide(down_buf[z])).astype(jnp.bfloat16)

    @pl.when(z == depth - 1)
    def _():
        z_copy(z, True).wait_recv()
        out_ref[...] = (total + wide(up_buf[z])).astype(jnp.bfloat16)

    @pl.when((z > 0) & (z < depth - 1))
    def _():
        z_copy(z, True).wait_recv()
        z_copy(z, False).wait_recv()
        out_ref[...] = (total + wide(up_buf[z]) + wide(down_buf[z])).astype(jnp.bfloat16)

    def drain(step):
        at = z + step
        core_copy(at, True).wait_send()
        core_copy(at, False).wait_send()
        copy(side, step, o).wait_send()
        copy(core, step, o).wait_send()
        copy(core, step, across).wait_send()
        if step != 0:
            z_copy(at, step > 0).wait_send()
        if 1 - depth < step <= 0:
            @pl.when(z < depth - 1)
            def _():
                copy(up, step, o).wait_send()
        if 0 <= step < depth - 1:
            @pl.when(z > 0)
            def _():
                copy(down, step, o).wait_send()

    drain(0)
    for step, there in order:
        pl.when(there)(functools.partial(drain, step))


UNROLL = 2


def small_body(psi, left_env, right_env, sec_tiles, task_sector, task_term, task_live):
    depth = lax.axis_size("task")
    span = left_env.shape[-1]
    rows, columns = psi.shape
    env = left_env.reshape(-1, depth, span, span)
    right = right_env[0]
    pairs = env.shape[0]
    unit = math.gcd(rows, TILE)
    operands = (psi.reshape(-1, unit, columns), env, right, sec_tiles, task_sector, task_term, task_live)
    dma, vmem, smem = pltpu.SemaphoreType.DMA, pltpu.VMEM, pltpu.SMEM
    blocks = vmem((depth, rows, columns), jnp.bfloat16)
    ints = [smem(a.shape, jnp.int32) for a in operands[3:]]
    return pl.pallas_call(
        functools.partial(whole_kernel, depth),
        out_shape=jax.ShapeDtypeStruct(psi.shape, jnp.bfloat16),
        in_specs=[pl.BlockSpec(memory_space=pl.ANY)] * len(operands),
        out_specs=pl.BlockSpec(memory_space=pltpu.VMEM),
        scratch_shapes=[vmem((4 * rows // unit, unit, columns), jnp.bfloat16)] * (2 * depth - 1)
        + [vmem(env.shape, env.dtype), vmem(right.shape, right.dtype)] + ints
        + [smem((pairs,), jnp.int32)] * 2
        + [vmem((pairs, span // TILE, TILE, columns), jnp.bfloat16), vmem((depth, 4 * rows, columns), jnp.bfloat16),
           vmem((2, depth, rows, columns), jnp.bfloat16)] + [blocks] * 5
        + [dma((4, depth * 4)), dma((depth * 4,)), dma((len(operands),)), dma((2, depth)), dma((depth,)),
           dma((depth,)), dma((2, depth)), dma((depth,)), dma((depth,)), dma((depth,))],
        compiler_params=pltpu.CompilerParams(
            collective_id=0, has_side_effects=True, vmem_limit_bytes=VMEM_LIMIT
        ),
    )(*operands)


def solution(mesh):
    paired = mesh.shape["ops"] == 4 and mesh.shape["task"] <= 4
    return jax.shard_map(
        small_body if paired else body,
        mesh=mesh,
        in_specs=(
            P(("copies", "task", "ops"), None),
            P(("copies", "ops"), "task", None, None, None),
            P(("copies", "ops"), None, None, None),
            P("copies", None),
            P("copies", None),
            P("copies", None),
            P(("copies", "ops"), None, None),
        ),
        out_specs=P(("copies", "task", "ops"), None),
        check_vma=False,
    )
```

```python
import functools
import math

import jax
import jax.numpy as jnp
from jax import lax
from jax.experimental import pallas as pl
from jax.experimental.pallas import tpu as pltpu
from jax.sharding import PartitionSpec as P

TILE = 128
MR = 128
NV = 3


def lookup(entries, selected):
    sector_marks = selected[..., None] == jnp.arange(entries.shape[-1])
    return jnp.sum(jnp.where(sector_marks, entries, 0), axis=-1)


def apply_terms(blocks, pieces, pattern, keep_rows, term_ids, live_flags, right_blocks):
    mixed_rows = jnp.einsum(pattern, blocks, pieces, preferred_element_type=jnp.float32)
    mixed_rows = jnp.where(keep_rows[..., None], mixed_rows, 0.0).astype(jnp.bfloat16)
    leading = mixed_rows.shape[:3]
    per_vector = mixed_rows.reshape(leading + (NV, MR))
    chosen = right_blocks[term_ids]
    result = jnp.einsum("abrvm,abmn->abrvn", per_vector, chosen, preferred_element_type=jnp.float32)
    result = result * live_flags[:, :, None, None, None].astype(jnp.float32)
    return result.reshape(leading + (NV * MR,)).astype(jnp.bfloat16)


def body(psi, left_env, right_env, sec_tiles, task_sector, task_term, task_live):
    owners = lax.axis_size("task")
    owner_index = lax.axis_index("task")
    columns = psi.shape[1]
    span_rows = left_env.shape[-1]
    slot_count = task_sector.shape[1]
    pair_count = slot_count // owners
    sector_count = sec_tiles.shape[1]
    own_block = lax.all_gather(psi, "ops", axis=0, tiled=True)
    own_rows = own_block.shape[0]
    sector_rows = lax.dynamic_index_in_dim(sec_tiles, owner_index, 0, keepdims=False) * TILE
    starts = jnp.cumsum(sector_rows) - sector_rows
    padded = jnp.concatenate([own_block, jnp.zeros((span_rows, columns), own_block.dtype)], axis=0)
    offsets = jnp.arange(span_rows)
    sent_sector = lax.dynamic_index_in_dim(
        task_sector.reshape(owners, pair_count, owners), owner_index, 2, keepdims=False
    )
    counts = lookup(sector_rows, sent_sector)
    begins = lookup(starts, sent_sector)
    send_keep = offsets < counts[..., None]
    row_ids = begins[..., None] + offsets
    pieces = jnp.where(send_keep[..., None], padded[row_ids], jnp.zeros((), own_block.dtype))
    group_live = task_live[0]
    right_blocks = right_env[0]
    arrived = lax.all_to_all(pieces, "task", split_axis=0, concat_axis=0, tiled=True)
    my_sectors = lax.dynamic_index_in_dim(task_sector, owner_index, 0, keepdims=False).reshape(
        pair_count, owners
    )
    all_rows = sec_tiles * TILE
    slot_rows = lookup(all_rows[None, :, :], my_sectors)
    own_keep = offsets < slot_rows[..., None]
    term_ids = lax.dynamic_index_in_dim(task_term, owner_index, 0, keepdims=False).reshape(
        pair_count, owners
    )
    live_flags = lax.dynamic_index_in_dim(group_live, owner_index, 0, keepdims=False).reshape(
        pair_count, owners
    )
    blocks = left_env.reshape(pair_count, owners, span_rows, span_rows)
    result = apply_terms(
        blocks, arrived, "tirs,itsc->tirc", own_keep, term_ids, live_flags, right_blocks
    )
    returned = lax.all_to_all(result, "task", split_axis=1, concat_axis=1, tiled=True)
    sum_pattern = "jtl,tjrc->lrc"
    sector_marks = (sent_sector[..., None] == jnp.arange(sector_count)).astype(jnp.bfloat16)
    sector_sums = jnp.einsum(
        sum_pattern, sector_marks, returned, preferred_element_type=jnp.float32
    )
    placed = jnp.zeros((own_rows + span_rows, columns), jnp.float32)
    for sector in range(sector_count):
        placed = lax.dynamic_update_slice_in_dim(placed, sector_sums[sector], starts[sector], 0)
    summed = lax.psum_scatter(placed[:own_rows], "ops", scatter_dimension=0, tiled=True)
    return summed.astype(jnp.bfloat16)


MESH = pl.DeviceIdType.MESH
VMEM_LIMIT = 60 * 1024 * 1024


def place():
    z = lax.axis_index("task")
    o = lax.axis_index("ops")
    across = lax.rem(o + 2, 4)
    sibling = o + 1 - 2 * lax.rem(o, 2)
    return z, o, across, sibling


def enter(z, across, sibling, depth):
    barrier = pltpu.get_barrier_semaphore()

    def greet(**where):
        pl.semaphore_signal(barrier, inc=1, device_id=where, device_id_type=MESH)

    greet(ops=across)
    greet(ops=sibling)

    @pl.when(z > 0)
    def _():
        greet(task=z - 1)

    @pl.when(z < depth - 1)
    def _():
        greet(task=z + 1)

    inner = jnp.where(z > 0, 1, 0) + jnp.where(z < depth - 1, 1, 0)
    pl.semaphore_wait(barrier, 2 + inner)


def whole_kernel(depth, psi_ref, env_ref, right_ref, tiles_ref, sector_ref, term_ref, live_ref, out_ref, *scratch):
    steps = 2 * depth - 1
    homes, scratch = scratch[:steps], scratch[steps:]
    (env, right, tiles, sector, term, live, first_tile, end_tile, mixed, part, core_buf, side_buf, up_buf, down_buf,
     side_out, z_out, send_sem, recv_sem, local_sem, core_send, side_send, z_send,
     core_recv, side_recv, up_recv, down_recv) = scratch
    z, o, across, sibling = place()
    other = lax.rem(sibling + 2, 4)
    pairs = env.shape[0]
    units, unit = psi_ref.shape[:2]
    rows = units * unit
    chunk_units = units // CHUNKS
    chunk_rows = rows // CHUNKS
    per_tile = TILE // unit
    own_tiles = homes[0].shape[0] // per_tile
    sectors = tiles.shape[1]
    up, down, side, core = 0, 1, 2, 3

    def block(step, col, chunk):
        return homes[step + depth - 1].at[pl.ds(col * units + chunk * chunk_units, chunk_units)]

    def within(chunk):
        return pl.ds(chunk * chunk_rows, chunk_rows)

    loads = [
        pltpu.make_async_copy(source, target, local_sem.at[i])
        for i, (source, target) in enumerate((
            (psi_ref, homes[depth - 1].at[pl.ds(o * units, units)]), (tiles_ref, tiles), (sector_ref, sector), (term_ref, term), (live_ref, live),
            (right_ref, right), (env_ref, env),
        ))
    ]
    for load in loads:
        load.start()
    enter(z, across, sibling, depth)

    def copy(way, step, col, chunk):
        shift = (-1, 1, 0, 0)[way]
        where = ({"task": z + 1}, {"task": z - 1}, {"ops": across}, {"ops": sibling})[way]
        index = ((z + step) * 4 + col) * CHUNKS + chunk
        own = step == 0 and col is o
        return pltpu.make_async_remote_copy(
            src_ref=psi_ref.at[pl.ds(chunk * chunk_units, chunk_units)] if own else block(step, col, chunk),
            dst_ref=block(step + shift, col, chunk),
            send_sem=send_sem.at[way, index],
            recv_sem=recv_sem.at[index],
            device_id=where,
            device_id_type=MESH,
        )

    def arrived(step, col, chunk):
        copy(core, step, col, chunk).wait_recv()

    def offsets(t):
        return ((-t, z - t >= 0), (t, z + t <= depth - 1))

    def core_copy(at, far):
        col = other if far else sibling
        return pltpu.make_async_remote_copy(
            src_ref=part.at[at, pl.ds(pl.multiple_of(col * rows, 16), rows)],
            dst_ref=core_buf.at[int(far), at],
            send_sem=core_send.at[int(far), at],
            recv_sem=core_recv.at[int(far), at],
            device_id={"ops": sibling},
            device_id_type=MESH,
        )

    def side_copy(at, chunk):
        return pltpu.make_async_remote_copy(
            src_ref=side_out.at[at, within(chunk)],
            dst_ref=side_buf.at[at, within(chunk)],
            send_sem=side_send.at[at, chunk],
            recv_sem=side_recv.at[at, chunk],
            device_id={"ops": across},
            device_id_type=MESH,
        )

    def z_copy(at, rising, chunk):
        return pltpu.make_async_remote_copy(
            src_ref=z_out.at[at, within(chunk)],
            dst_ref=(up_buf if rising else down_buf).at[at, within(chunk)],
            send_sem=z_send.at[at, chunk],
            recv_sem=(up_recv if rising else down_recv).at[at, chunk],
            device_id={"task": z + 1 if rising else z - 1},
            device_id_type=MESH,
        )

    def wide(value):
        return value.astype(jnp.float32)

    def part_rows(at, col, chunk):
        return wide(part[at, pl.ds(pl.multiple_of(col * rows + chunk * chunk_rows, 16), chunk_rows), :])

    def apply_home(step):
        home = z + step
        held = homes[step + depth - 1]

        def one_slot(pair, _):
            slot = pair * depth + home
            which = sector[z, slot]
            start = jnp.int32(0)
            for earlier in range(sectors - 1):
                start += jnp.where(earlier < which, tiles[home, earlier], 0)
            count = tiles[home, which]
            first_tile[pair] = start
            end_tile[pair] = jnp.where(live[0, z, slot] != 0, start + count, start)
            next_tile = jnp.minimum(start + 1, own_tiles - 1)
            pieces = [held[start * per_tile + i] for i in range(per_tile)]
            for i in range(per_tile):
                piece = held[next_tile * per_tile + i]
                pieces.append(jnp.where(count > 1, piece, jnp.zeros_like(piece)))
            rows_in = jnp.concatenate(pieces, axis=0)
            turned = jnp.dot(env[pair, home], rows_in, preferred_element_type=jnp.float32).astype(jnp.bfloat16)
            chosen = right[term[z, slot]]
            for v in range(NV):
                cols = slice(v * MR, (v + 1) * MR)
                result = jnp.dot(
                    turned[:, cols], chosen, preferred_element_type=jnp.float32
                ).astype(jnp.bfloat16)
                mixed[pair, 0, :, cols] = result[:TILE]
                mixed[pair, 1, :, cols] = result[TILE:]
            return 0

        lax.fori_loop(0, pairs, one_slot, 0, unroll=UNROLL)

        def one_tile(tile, _):
            for v in range(NV):
                cols = slice(v * MR, (v + 1) * MR)
                total = jnp.zeros((TILE, MR), jnp.float32)
                for pair in range(pairs):
                    start, end = first_tile[pair], end_tile[pair]
                    weight = jnp.where((tile >= start) & (tile < end), 1.0, 0.0)
                    offset = jnp.where(tile > start, 1, 0)
                    total += weight * wide(mixed[pair, offset, :, cols])
                part[home, pl.ds(pl.multiple_of(tile * TILE, TILE), TILE), cols] = total.astype(jnp.bfloat16)
            return 0

        lax.fori_loop(0, own_tiles, one_tile, 0)
        core_copy(home, True).start()
        core_copy(home, False).start()

    def finish_home(step):
        for chunk in range(CHUNKS):
            arrived(step, across, chunk)
            copy(core, step, across, chunk).start()
        for chunk in range(CHUNKS):
            arrived(step, sibling, chunk)
            arrived(step, other, chunk)
        apply_home(step)

    def send_side(at):
        core_copy(at, True).wait_recv()
        for chunk in range(CHUNKS):
            side_out[at, within(chunk), :] = (
                part_rows(at, across, chunk) + wide(core_buf[1, at, within(chunk), :])
            ).astype(jnp.bfloat16)
            side_copy(at, chunk).start()

    def gathered(at, chunk):
        if chunk == 0:
            core_copy(at, False).wait_recv()
        side_copy(at, chunk).wait_recv()
        return part_rows(at, o, chunk) + wide(core_buf[0, at, within(chunk), :]) + wide(side_buf[at, within(chunk), :])

    def send_z(step):
        at = z + step
        rising = step > 0
        buf = up_buf if rising else down_buf
        first = (z == 0) if rising else (z == depth - 1)

        @pl.when(first)
        def _():
            for chunk in range(CHUNKS):
                z_out[at, within(chunk), :] = gathered(at, chunk).astype(jnp.bfloat16)
                z_copy(at, rising, chunk).start()

        @pl.when(jnp.logical_not(first))
        def _():
            for chunk in range(CHUNKS):
                total = gathered(at, chunk)
                z_copy(at, rising, chunk).wait_recv()
                z_out[at, within(chunk), :] = (total + wide(buf[at, within(chunk), :])).astype(jnp.bfloat16)
                z_copy(at, rising, chunk).start()

    for chunk in range(CHUNKS):
        @pl.when(z < depth - 1)
        def _():
            copy(up, 0, o, chunk).start()

        @pl.when(z > 0)
        def _():
            copy(down, 0, o, chunk).start()

        copy(side, 0, o, chunk).start()
        copy(core, 0, o, chunk).start()

    def forward(t):
        for chunk in range(CHUNKS):
            for step, there in offsets(t):
                @pl.when(there)
                def _():
                    arrived(step, o, chunk)

                    if 1 - depth < step < 0:
                        @pl.when(z < depth - 1)
                        def _():
                            copy(up, step, o, chunk).start()
                    if 0 < step < depth - 1:
                        @pl.when(z > 0)
                        def _():
                            copy(down, step, o, chunk).start()

                    copy(side, step, o, chunk).start()
                    copy(core, step, o, chunk).start()

    forward(1)
    for load in loads:
        load.wait()
    finish_home(0)
    for t in range(1, depth):
        if t + 1 < depth:
            forward(t + 1)
        if 2 * t >= depth - 1:
            @pl.when(jnp.maximum(z, depth - 1 - z) == t)
            def _():
                send_side(z)
        for step, there in offsets(t):
            pl.when(there)(functools.partial(finish_home, step))
    order = []
    for t in range(depth - 1, 0, -1):
        order += offsets(t)[::-1]
    for step, there in order:
        pl.when(there)(functools.partial(send_side, z + step))
    for step, there in order:
        pl.when(there)(functools.partial(send_z, step))

    def finish(chunk, below, above):
        total = gathered(z, chunk)
        if below:
            z_copy(z, True, chunk).wait_recv()
            total += wide(up_buf[z, within(chunk), :])
        if above:
            z_copy(z, False, chunk).wait_recv()
            total += wide(down_buf[z, within(chunk), :])
        out_ref[within(chunk), :] = total.astype(jnp.bfloat16)

    for below, above, here in (
        (False, True, z == 0), (True, False, z == depth - 1), (True, True, (z > 0) & (z < depth - 1))
    ):
        @pl.when(here)
        def _():
            for chunk in range(CHUNKS):
                finish(chunk, below, above)

    def drain(step):
        at = z + step
        core_copy(at, True).wait_send()
        core_copy(at, False).wait_send()
        for chunk in range(CHUNKS):
            side_copy(at, chunk).wait_send()
            copy(side, step, o, chunk).wait_send()
            copy(core, step, o, chunk).wait_send()
            copy(core, step, across, chunk).wait_send()
            if step != 0:
                z_copy(at, step > 0, chunk).wait_send()
            if 1 - depth < step <= 0:
                @pl.when(z < depth - 1)
                def _():
                    copy(up, step, o, chunk).wait_send()
            if 0 <= step < depth - 1:
                @pl.when(z > 0)
                def _():
                    copy(down, step, o, chunk).wait_send()

    drain(0)
    for step, there in order:
        pl.when(there)(functools.partial(drain, step))


UNROLL = 2
CHUNKS = 2


def small_body(psi, left_env, right_env, sec_tiles, task_sector, task_term, task_live):
    depth = lax.axis_size("task")
    span = left_env.shape[-1]
    rows, columns = psi.shape
    env = left_env.reshape(-1, depth, span, span)
    right = right_env[0]
    pairs = env.shape[0]
    unit = math.gcd(rows // CHUNKS, TILE)
    operands = (psi.reshape(-1, unit, columns), env, right, sec_tiles, task_sector, task_term, task_live)
    dma, vmem, smem = pltpu.SemaphoreType.DMA, pltpu.VMEM, pltpu.SMEM
    blocks = vmem((depth, rows, columns), jnp.bfloat16)
    ints = [smem(a.shape, jnp.int32) for a in operands[3:]]
    return pl.pallas_call(
        functools.partial(whole_kernel, depth),
        out_shape=jax.ShapeDtypeStruct(psi.shape, jnp.bfloat16),
        in_specs=[pl.BlockSpec(memory_space=pl.ANY)] * len(operands),
        out_specs=pl.BlockSpec(memory_space=pltpu.VMEM),
        scratch_shapes=[vmem((4 * rows // unit, unit, columns), jnp.bfloat16)] * (2 * depth - 1)
        + [vmem(env.shape, env.dtype), vmem(right.shape, right.dtype)] + ints
        + [smem((pairs,), jnp.int32)] * 2
        + [vmem((pairs, span // TILE, TILE, columns), jnp.bfloat16), vmem((depth, 4 * rows, columns), jnp.bfloat16),
           vmem((2, depth, rows, columns), jnp.bfloat16)] + [blocks] * 5
        + [dma((4, depth * 4 * CHUNKS)), dma((depth * 4 * CHUNKS,)), dma((len(operands),)), dma((2, depth))]
        + [dma((depth, CHUNKS))] * 2 + [dma((2, depth))] + [dma((depth, CHUNKS))] * 3,
        compiler_params=pltpu.CompilerParams(
            collective_id=0, has_side_effects=True, vmem_limit_bytes=VMEM_LIMIT
        ),
    )(*operands)


def solution(mesh):
    paired = mesh.shape["ops"] == 4 and mesh.shape["task"] <= 4
    return jax.shard_map(
        small_body if paired else body,
        mesh=mesh,
        in_specs=(
            P(("copies", "task", "ops"), None),
            P(("copies", "ops"), "task", None, None, None),
            P(("copies", "ops"), None, None, None),
            P("copies", None),
            P("copies", None),
            P("copies", None),
            P(("copies", "ops"), None, None),
        ),
        out_specs=P(("copies", "task", "ops"), None),
        check_vma=False,
    )
```

```python
import functools
import math

import jax
import jax.numpy as jnp
from jax import lax
from jax.experimental import pallas as pl
from jax.experimental.pallas import tpu as pltpu
from jax.sharding import PartitionSpec as P

TILE = 128
MR = 128
NV = 3


def lookup(entries, selected):
    sector_marks = selected[..., None] == jnp.arange(entries.shape[-1])
    return jnp.sum(jnp.where(sector_marks, entries, 0), axis=-1)


def apply_terms(blocks, pieces, pattern, keep_rows, term_ids, live_flags, right_blocks):
    mixed_rows = jnp.einsum(pattern, blocks, pieces, preferred_element_type=jnp.float32)
    mixed_rows = jnp.where(keep_rows[..., None], mixed_rows, 0.0).astype(jnp.bfloat16)
    leading = mixed_rows.shape[:3]
    per_vector = mixed_rows.reshape(leading + (NV, MR))
    chosen = right_blocks[term_ids]
    result = jnp.einsum("abrvm,abmn->abrvn", per_vector, chosen, preferred_element_type=jnp.float32)
    result = result * live_flags[:, :, None, None, None].astype(jnp.float32)
    return result.reshape(leading + (NV * MR,)).astype(jnp.bfloat16)


def body(psi, left_env, right_env, sec_tiles, task_sector, task_term, task_live):
    owners = lax.axis_size("task")
    owner_index = lax.axis_index("task")
    columns = psi.shape[1]
    span_rows = left_env.shape[-1]
    slot_count = task_sector.shape[1]
    pair_count = slot_count // owners
    sector_count = sec_tiles.shape[1]
    own_block = lax.all_gather(psi, "ops", axis=0, tiled=True)
    own_rows = own_block.shape[0]
    sector_rows = lax.dynamic_index_in_dim(sec_tiles, owner_index, 0, keepdims=False) * TILE
    starts = jnp.cumsum(sector_rows) - sector_rows
    padded = jnp.concatenate([own_block, jnp.zeros((span_rows, columns), own_block.dtype)], axis=0)
    offsets = jnp.arange(span_rows)
    sent_sector = lax.dynamic_index_in_dim(
        task_sector.reshape(owners, pair_count, owners), owner_index, 2, keepdims=False
    )
    counts = lookup(sector_rows, sent_sector)
    begins = lookup(starts, sent_sector)
    send_keep = offsets < counts[..., None]
    row_ids = begins[..., None] + offsets
    pieces = jnp.where(send_keep[..., None], padded[row_ids], jnp.zeros((), own_block.dtype))
    group_live = task_live[0]
    right_blocks = right_env[0]
    arrived = lax.all_to_all(pieces, "task", split_axis=0, concat_axis=0, tiled=True)
    my_sectors = lax.dynamic_index_in_dim(task_sector, owner_index, 0, keepdims=False).reshape(
        pair_count, owners
    )
    all_rows = sec_tiles * TILE
    slot_rows = lookup(all_rows[None, :, :], my_sectors)
    own_keep = offsets < slot_rows[..., None]
    term_ids = lax.dynamic_index_in_dim(task_term, owner_index, 0, keepdims=False).reshape(
        pair_count, owners
    )
    live_flags = lax.dynamic_index_in_dim(group_live, owner_index, 0, keepdims=False).reshape(
        pair_count, owners
    )
    blocks = left_env.reshape(pair_count, owners, span_rows, span_rows)
    result = apply_terms(
        blocks, arrived, "tirs,itsc->tirc", own_keep, term_ids, live_flags, right_blocks
    )
    returned = lax.all_to_all(result, "task", split_axis=1, concat_axis=1, tiled=True)
    sum_pattern = "jtl,tjrc->lrc"
    sector_marks = (sent_sector[..., None] == jnp.arange(sector_count)).astype(jnp.bfloat16)
    sector_sums = jnp.einsum(
        sum_pattern, sector_marks, returned, preferred_element_type=jnp.float32
    )
    placed = jnp.zeros((own_rows + span_rows, columns), jnp.float32)
    for sector in range(sector_count):
        placed = lax.dynamic_update_slice_in_dim(placed, sector_sums[sector], starts[sector], 0)
    summed = lax.psum_scatter(placed[:own_rows], "ops", scatter_dimension=0, tiled=True)
    return summed.astype(jnp.bfloat16)


MESH = pl.DeviceIdType.MESH
VMEM_LIMIT = 60 * 1024 * 1024


def place():
    z = lax.axis_index("task")
    o = lax.axis_index("ops")
    across = lax.rem(o + 2, 4)
    sibling = o + 1 - 2 * lax.rem(o, 2)
    return z, o, across, sibling


def enter(z, across, sibling, depth):
    barrier = pltpu.get_barrier_semaphore()

    def greet(**where):
        pl.semaphore_signal(barrier, inc=1, device_id=where, device_id_type=MESH)

    greet(ops=across)
    greet(ops=sibling)

    @pl.when(z > 0)
    def _():
        greet(task=z - 1)

    @pl.when(z < depth - 1)
    def _():
        greet(task=z + 1)

    inner = jnp.where(z > 0, 1, 0) + jnp.where(z < depth - 1, 1, 0)
    pl.semaphore_wait(barrier, 2 + inner)


def whole_kernel(depth, psi_ref, env_ref, right_ref, tiles_ref, sector_ref, term_ref, live_ref, out_ref, *scratch):
    steps = 2 * depth - 1
    homes, scratch = scratch[:steps], scratch[steps:]
    (env, right, tiles, sector, term, live, first_tile, end_tile, mixed, part, core_buf, side_buf, up_buf, down_buf,
     side_out, z_out, send_sem, recv_sem, local_sem, core_send, side_send, z_send,
     core_recv, side_recv, up_recv, down_recv) = scratch
    z, o, across, sibling = place()
    other = lax.rem(sibling + 2, 4)
    pairs, span = env.shape[0], env.shape[-1]
    units, unit = psi_ref.shape[:2]
    rows = units * unit
    chunk_units = units // CHUNKS
    chunk_rows = rows // CHUNKS
    per_tile = TILE // unit
    own_tiles = homes[0].shape[0] // per_tile
    sectors = tiles.shape[1]
    up, down, side, core = 0, 1, 2, 3

    def block(step, col, chunk):
        return homes[step + depth - 1].at[pl.ds(col * units + chunk * chunk_units, chunk_units)]

    def within(chunk):
        return pl.ds(chunk * chunk_rows, chunk_rows)

    loads = [
        pltpu.make_async_copy(source, target, local_sem.at[i])
        for i, (source, target) in enumerate((
            (psi_ref, homes[depth - 1].at[pl.ds(o * units, units)]), (tiles_ref, tiles), (sector_ref, sector), (term_ref, term), (live_ref, live),
            (right_ref, right), (env_ref, env),
        ))
    ]
    for load in loads:
        load.start()
    enter(z, across, sibling, depth)

    def copy(way, step, col, chunk):
        shift = (-1, 1, 0, 0)[way]
        where = ({"task": z + 1}, {"task": z - 1}, {"ops": across}, {"ops": sibling})[way]
        index = ((z + step) * 4 + col) * CHUNKS + chunk
        own = step == 0 and col is o
        return pltpu.make_async_remote_copy(
            src_ref=psi_ref.at[pl.ds(chunk * chunk_units, chunk_units)] if own else block(step, col, chunk),
            dst_ref=block(step + shift, col, chunk),
            send_sem=send_sem.at[way, index],
            recv_sem=recv_sem.at[index],
            device_id=where,
            device_id_type=MESH,
        )

    def arrived(step, col, chunk):
        copy(core, step, col, chunk).wait_recv()

    def offsets(t):
        return ((-t, z - t >= 0), (t, z + t <= depth - 1))

    def core_copy(at, far):
        col = other if far else sibling
        return pltpu.make_async_remote_copy(
            src_ref=part.at[at, pl.ds(pl.multiple_of(col * rows, 16), rows)],
            dst_ref=core_buf.at[int(far), at],
            send_sem=core_send.at[int(far), at],
            recv_sem=core_recv.at[int(far), at],
            device_id={"ops": sibling},
            device_id_type=MESH,
        )

    def side_copy(at, chunk):
        return pltpu.make_async_remote_copy(
            src_ref=side_out.at[at, within(chunk)],
            dst_ref=side_buf.at[at, within(chunk)],
            send_sem=side_send.at[at, chunk],
            recv_sem=side_recv.at[at, chunk],
            device_id={"ops": across},
            device_id_type=MESH,
        )

    def z_copy(at, rising, chunk):
        return pltpu.make_async_remote_copy(
            src_ref=z_out.at[at, within(chunk)],
            dst_ref=(up_buf if rising else down_buf).at[at, within(chunk)],
            send_sem=z_send.at[at, chunk],
            recv_sem=(up_recv if rising else down_recv).at[at, chunk],
            device_id={"task": z + 1 if rising else z - 1},
            device_id_type=MESH,
        )

    def wide(value):
        return value.astype(jnp.float32)

    def part_rows(at, col, chunk):
        return wide(part[at, pl.ds(pl.multiple_of(col * rows + chunk * chunk_rows, 16), chunk_rows), :])

    def apply_home(step):
        home = z + step
        held = homes[step + depth - 1]

        def one_slot(pair, _):
            slot = pair * depth + home
            which = sector[z, slot]
            start = jnp.int32(0)
            for earlier in range(sectors - 1):
                start += jnp.where(earlier < which, tiles[home, earlier], 0)
            count = tiles[home, which]
            first_tile[pair] = start
            end_tile[pair] = jnp.where(live[0, z, slot] != 0, start + count, start)
            next_tile = jnp.minimum(start + 1, own_tiles - 1)
            pieces = [held[start * per_tile + i] for i in range(per_tile)]
            for i in range(per_tile):
                piece = held[next_tile * per_tile + i]
                pieces.append(jnp.where(count > 1, piece, jnp.zeros_like(piece)))
            rows_in = jnp.concatenate(pieces, axis=0)
            turned = jnp.dot(env[pair, home], rows_in, preferred_element_type=jnp.float32).astype(jnp.bfloat16)
            chosen = right[term[z, slot]]
            stacked = jnp.concatenate([turned[:, v * MR:(v + 1) * MR] for v in range(NV)], axis=0)
            result = jnp.dot(stacked, chosen, preferred_element_type=jnp.float32).astype(jnp.bfloat16)
            for v in range(NV):
                for half in range(span // TILE):
                    at_row = v * span + half * TILE
                    mixed[pair, half, :, v * MR:(v + 1) * MR] = result[at_row:at_row + TILE]
            return 0

        lax.fori_loop(0, pairs, one_slot, 0, unroll=UNROLL)

        def one_tile(tile, _):
            for v in range(NV):
                cols = slice(v * MR, (v + 1) * MR)
                total = jnp.zeros((TILE, MR), jnp.float32)
                for pair in range(pairs):
                    start, end = first_tile[pair], end_tile[pair]
                    weight = jnp.where((tile >= start) & (tile < end), 1.0, 0.0)
                    offset = jnp.where(tile > start, 1, 0)
                    total += weight * wide(mixed[pair, offset, :, cols])
                part[home, pl.ds(pl.multiple_of(tile * TILE, TILE), TILE), cols] = total.astype(jnp.bfloat16)
            return 0

        lax.fori_loop(0, own_tiles, one_tile, 0)
        core_copy(home, True).start()
        core_copy(home, False).start()

    def finish_home(step):
        for chunk in range(CHUNKS):
            arrived(step, across, chunk)
            copy(core, step, across, chunk).start()
        for chunk in range(CHUNKS):
            arrived(step, sibling, chunk)
            arrived(step, other, chunk)
        apply_home(step)

    def send_side(at):
        core_copy(at, True).wait_recv()
        for chunk in range(CHUNKS):
            side_out[at, within(chunk), :] = (
                part_rows(at, across, chunk) + wide(core_buf[1, at, within(chunk), :])
            ).astype(jnp.bfloat16)
            side_copy(at, chunk).start()

    def gathered(at, chunk):
        if chunk == 0:
            core_copy(at, False).wait_recv()
        side_copy(at, chunk).wait_recv()
        return part_rows(at, o, chunk) + wide(core_buf[0, at, within(chunk), :]) + wide(side_buf[at, within(chunk), :])

    def send_z(step):
        at = z + step
        rising = step > 0
        buf = up_buf if rising else down_buf
        first = (z == 0) if rising else (z == depth - 1)

        @pl.when(first)
        def _():
            for chunk in range(CHUNKS):
                z_out[at, within(chunk), :] = gathered(at, chunk).astype(jnp.bfloat16)
                z_copy(at, rising, chunk).start()

        @pl.when(jnp.logical_not(first))
        def _():
            for chunk in range(CHUNKS):
                total = gathered(at, chunk)
                z_copy(at, rising, chunk).wait_recv()
                z_out[at, within(chunk), :] = (total + wide(buf[at, within(chunk), :])).astype(jnp.bfloat16)
                z_copy(at, rising, chunk).start()

    for chunk in range(CHUNKS):
        @pl.when(z < depth - 1)
        def _():
            copy(up, 0, o, chunk).start()

        @pl.when(z > 0)
        def _():
            copy(down, 0, o, chunk).start()

        copy(side, 0, o, chunk).start()
        copy(core, 0, o, chunk).start()

    def forward(t):
        for chunk in range(CHUNKS):
            for step, there in offsets(t):
                @pl.when(there)
                def _():
                    arrived(step, o, chunk)

                    if 1 - depth < step < 0:
                        @pl.when(z < depth - 1)
                        def _():
                            copy(up, step, o, chunk).start()
                    if 0 < step < depth - 1:
                        @pl.when(z > 0)
                        def _():
                            copy(down, step, o, chunk).start()

                    copy(side, step, o, chunk).start()
                    copy(core, step, o, chunk).start()

    forward(1)
    for load in loads:
        load.wait()
    finish_home(0)
    for t in range(1, depth):
        if t + 1 < depth:
            forward(t + 1)
        if 2 * t >= depth - 1:
            @pl.when(jnp.maximum(z, depth - 1 - z) == t)
            def _():
                send_side(z)
        for step, there in offsets(t):
            pl.when(there)(functools.partial(finish_home, step))
    order = []
    for t in range(depth - 1, 0, -1):
        order += offsets(t)[::-1]
    for step, there in order:
        pl.when(there)(functools.partial(send_side, z + step))
    for step, there in order:
        pl.when(there)(functools.partial(send_z, step))

    def finish(chunk, below, above):
        total = gathered(z, chunk)
        if below:
            z_copy(z, True, chunk).wait_recv()
            total += wide(up_buf[z, within(chunk), :])
        if above:
            z_copy(z, False, chunk).wait_recv()
            total += wide(down_buf[z, within(chunk), :])
        out_ref[within(chunk), :] = total.astype(jnp.bfloat16)

    for below, above, here in (
        (False, True, z == 0), (True, False, z == depth - 1), (True, True, (z > 0) & (z < depth - 1))
    ):
        @pl.when(here)
        def _():
            for chunk in range(CHUNKS):
                finish(chunk, below, above)

    def drain(step):
        at = z + step
        core_copy(at, True).wait_send()
        core_copy(at, False).wait_send()
        for chunk in range(CHUNKS):
            side_copy(at, chunk).wait_send()
            copy(side, step, o, chunk).wait_send()
            copy(core, step, o, chunk).wait_send()
            copy(core, step, across, chunk).wait_send()
            if step != 0:
                z_copy(at, step > 0, chunk).wait_send()
            if 1 - depth < step <= 0:
                @pl.when(z < depth - 1)
                def _():
                    copy(up, step, o, chunk).wait_send()
            if 0 <= step < depth - 1:
                @pl.when(z > 0)
                def _():
                    copy(down, step, o, chunk).wait_send()

    drain(0)
    for step, there in order:
        pl.when(there)(functools.partial(drain, step))


UNROLL = 4
CHUNKS = 2


def small_body(psi, left_env, right_env, sec_tiles, task_sector, task_term, task_live):
    depth = lax.axis_size("task")
    span = left_env.shape[-1]
    rows, columns = psi.shape
    env = left_env.reshape(-1, depth, span, span)
    right = right_env[0]
    pairs = env.shape[0]
    unit = math.gcd(rows // CHUNKS, TILE)
    operands = (psi.reshape(-1, unit, columns), env, right, sec_tiles, task_sector, task_term, task_live)
    dma, vmem, smem = pltpu.SemaphoreType.DMA, pltpu.VMEM, pltpu.SMEM
    blocks = vmem((depth, rows, columns), jnp.bfloat16)
    ints = [smem(a.shape, jnp.int32) for a in operands[3:]]
    return pl.pallas_call(
        functools.partial(whole_kernel, depth),
        out_shape=jax.ShapeDtypeStruct(psi.shape, jnp.bfloat16),
        in_specs=[pl.BlockSpec(memory_space=pl.ANY)] * len(operands),
        out_specs=pl.BlockSpec(memory_space=pltpu.VMEM),
        scratch_shapes=[vmem((4 * rows // unit, unit, columns), jnp.bfloat16)] * (2 * depth - 1)
        + [vmem(env.shape, env.dtype), vmem(right.shape, right.dtype)] + ints
        + [smem((pairs,), jnp.int32)] * 2
        + [vmem((pairs, span // TILE, TILE, columns), jnp.bfloat16), vmem((depth, 4 * rows, columns), jnp.bfloat16),
           vmem((2, depth, rows, columns), jnp.bfloat16)] + [blocks] * 5
        + [dma((4, depth * 4 * CHUNKS)), dma((depth * 4 * CHUNKS,)), dma((len(operands),)), dma((2, depth))]
        + [dma((depth, CHUNKS))] * 2 + [dma((2, depth))] + [dma((depth, CHUNKS))] * 3,
        compiler_params=pltpu.CompilerParams(
            collective_id=0, has_side_effects=True, vmem_limit_bytes=VMEM_LIMIT
        ),
    )(*operands)


def solution(mesh):
    paired = mesh.shape["ops"] == 4 and mesh.shape["task"] <= 4
    return jax.shard_map(
        small_body if paired else body,
        mesh=mesh,
        in_specs=(
            P(("copies", "task", "ops"), None),
            P(("copies", "ops"), "task", None, None, None),
            P(("copies", "ops"), None, None, None),
            P("copies", None),
            P("copies", None),
            P("copies", None),
            P(("copies", "ops"), None, None),
        ),
        out_specs=P(("copies", "task", "ops"), None),
        check_vma=False,
    )
```
